32 devices in a mesh: ctx: 4 (over z), exp: 8 (over y, x, core).
Axes of the slice: x: 2, y: 2, z: 4, core: 2. Of those that a mesh axis runs over, the one named last changes fastest.
Arguments:
- tokens: bfloat16 [4096, 2048], P(('ctx', 'exp')), may hold values from -6 to 6
- expert_ids: int32 [4096, 1], P(('ctx', 'exp')), may hold values from 0 to 7; in each aligned block of 128 rows (0 to 127, 128 to 255, ...) at most 20 rows name the same one
- gate_weights: float32 [4096, 1], P(('ctx', 'exp')), may hold values from 0.1 to 1
- weight_gate: bfloat16 [8, 2048, 1024], P('exp', 'ctx'), may hold values from -0.125 to 0.125
- weight_up: bfloat16 [8, 2048, 1024], P('exp', 'ctx'), may hold values from -0.125 to 0.125
- weight_down: bfloat16 [8, 1024, 2048], P('exp', None, 'ctx'), may hold values from -0.1875 to 0.1875
- attn_queries: bfloat16 [4096, 2048], P(('ctx', 'exp')), may hold values from -6 to 6
- attn_keys: bfloat16 [4096, 2048], P(('ctx', 'exp')), may hold values from -6 to 6
- grad_out: bfloat16 [4096, 2048], P('ctx', 'exp'), may hold values from -6 to 6
Outputs:
- grad_tokens: bfloat16 [4096, 2048], P(('ctx', 'exp'))
- grad_queries: bfloat16 [4096, 2048], P(('ctx', 'exp'))
- grad_keys: bfloat16 [4096, 2048], P(('ctx', 'exp'))
The draws below stay inside these ranges and needn't reach their ends.
Inputs may be any that keep to these rules, and one draw needn't show every extreme that they name: `expert_ids`: each row names one expert. Within each aligned block of 128 rows (the rows of one device), no expert is named more than 20 times, a bound that some block reaches.
All inputs are finite; a program needn't handle non-finite values.
Results may differ from the reference program's by a relative error of at most 0.0085.
Values may be sent and summed in bfloat16 or wider, within the bound.
No kernel may reach another device: no remote copies, remote signals or barrier semaphores. Data moves between devices by JAX's collectives and lax.ppermute only.
A program may use at most 64 MiB of HBM per device.

```python
import math
import jax
import jax.numpy as jnp
import numpy as np
from jax import lax

D = 2048
H = 1024
HEAD_DIM = 128
TOPK = 1
BLOCK = 512
TOK_DEV = 128
EXPERTS = 8
CAP = 20
TOKENS = 4096
N_CTX = 4
N_EXP = 8


def levels(stream_key, dims, pieces, least, top_value):
    factor_of, own = 1.0, jax.random.fold_in(stream_key, 6)
    for position, blocks in pieces:
        draws = jnp.exp(jax.random.uniform(jax.random.fold_in(own, position), (blocks,), jnp.float32, least / len(pieces), top_value / len(pieces)))
        factor_of = factor_of * jnp.repeat(draws, dims[position] // blocks).reshape([-1 if axis == position else 1 for axis in range(len(dims))])
    return factor_of


def deal_out(own_key, own, number, rows, amount, top, most, lean):
    order = jax.random.permutation(own_key, amount)
    heavy_load, usual = shares(amount, rows * top, most, lean, True), shares(amount, rows * top, most, lean, False)
    places = jnp.arange(amount)

    def named(tallies, rotation):
        used = int((tallies > 0).sum())
        fixed = max(1, used // 4)
        shifted = fixed + (places - fixed + rotation * (used - fixed)) % max(1, amount - fixed)
        return jnp.zeros((amount,), jnp.int32).at[order[jnp.where(places < fixed, places, shifted)]].set(jnp.asarray(tallies, jnp.int32))

    tallies = jnp.where(number % 4 == 0, named(heavy_load, number // 4), named(usual, number - number // 4 - 1))
    mixed = jax.random.permutation(jax.random.fold_in(own, 3), amount)
    giver, receiver = mixed[0:amount // 2 * 2:2], mixed[1:amount // 2 * 2:2]
    slack = jnp.minimum(tallies[giver] - 1, most - tallies[receiver]) // 2
    slack = jnp.where((giver == order[0]) | (receiver == order[0]) | (tallies[receiver] == 0), 0, jnp.maximum(slack, 0))
    shifted = jax.random.randint(jax.random.fold_in(own, 4), (amount // 2,), 0, 1 << 20) % (slack + 1)
    tallies = tallies.at[giver].add(-shifted).at[receiver].add(shifted)
    labels = jnp.searchsorted(jnp.cumsum(tallies), jnp.arange(rows * top), side="right").astype(jnp.int32)
    grid = labels.reshape(top, rows).T
    grid = grid[jax.random.permutation(jax.random.fold_in(own, 1), rows)]
    rotation = jax.random.randint(jax.random.fold_in(own, 2), (rows, 1), 0, top)
    return jnp.take_along_axis(grid, (jnp.arange(top)[None, :] + rotation) % top, axis=1)


def shares(count, total, bound, skew, full):
    loads = [(1 << 20) // math.isqrt(grade ** skew) + 1 for grade in range(1, count + 1)]
    largest = bound if full else min(bound, max(-(-total // count), total * loads[0] // sum(loads)))
    least = 1 if total - largest >= count - 1 else 0
    counts, spare = [largest] + [least] * (count - 1), total - largest - least * (count - 1)
    while spare > 0:
        candidates = [i for i in range(1, count) if counts[i] < largest] or [i for i in range(1, count) if counts[i] < bound]
        mass, budget = sum([loads[i] for i in candidates]), spare
        for i in candidates:
            extra = min(bound - counts[i], max(1, budget * loads[i] // mass), spare)
            counts[i] = counts[i] + extra
            spare = spare - extra
    return np.array(counts)


def bell_draw(own_key, dims, spread, bound, pieces=(), kind=jnp.bfloat16):
    result = spread * jax.random.normal(own_key, dims, jnp.float32)
    if pieces:
        result = result * levels(own_key, dims, pieces, -0.22, 0.18)
    return jnp.clip(result, -bound, bound).astype(kind)


def setup_inputs(seed: int = 0) -> dict:
    streams_of = jax.random.split(jax.random.key(seed), 10)
    tokens = bell_draw(streams_of[0], (TOKENS, D), 1.0, 6.0, ((0, 32),))
    expert_ids_keys = jax.random.split(jax.random.fold_in(streams_of[1], 1), TOKENS // TOK_DEV)
    expert_ids_turns = jax.random.permutation(jax.random.fold_in(streams_of[1], 3), TOKENS // TOK_DEV)
    expert_ids = jax.vmap(lambda own, number: deal_out(jax.random.fold_in(streams_of[1], 2), own, number, TOK_DEV, EXPERTS, TOPK, CAP, 2))(expert_ids_keys, expert_ids_turns).reshape((TOKENS, TOPK))
    gate_weights = jnp.clip(jnp.exp(math.log(1.0) - 2.3025851 * jax.random.uniform(streams_of[2], (TOKENS, TOPK), jnp.float32) ** levels(streams_of[2], (TOKENS, TOPK), ((0, 32),), -0.2, 0.2)), 0.1, 1.0)
    weight_gate = bell_draw(streams_of[3], (EXPERTS, D, H), D ** -0.5, 0.125, ((0, 8), (1, 4)))
    weight_up = bell_draw(streams_of[4], (EXPERTS, D, H), D ** -0.5, 0.125, ((0, 8), (1, 4)))
    weight_down = bell_draw(streams_of[5], (EXPERTS, H, D), H ** -0.5, 0.1875, ((0, 8), (2, 4)))
    attn_queries = bell_draw(streams_of[6], (TOKENS, D), 1.0, 6.0, ((0, 32),))
    attn_keys = bell_draw(streams_of[7], (TOKENS, D), 1.0, 6.0, ((0, 32),))
    grad_out = bell_draw(streams_of[8], (TOKENS, D), 1.0, 6.0, ((0, 4), (1, 8)))
    return {"tokens": tokens, "expert_ids": expert_ids, "gate_weights": gate_weights, "weight_gate": weight_gate, "weight_up": weight_up, "weight_down": weight_down, "attn_queries": attn_queries, "attn_keys": attn_keys, "grad_out": grad_out}


def silu_parts(gate_pre):
    sigmoid = jax.nn.sigmoid(gate_pre)
    activation = gate_pre * sigmoid
    silu_slope = sigmoid * (1.0 + gate_pre * (1.0 - sigmoid))
    return activation, silu_slope


def expert_forward(slot_rows, weight_one, weight_three, weight_two):
    gate_pre = jnp.dot(slot_rows, weight_one, preferred_element_type=jnp.float32)
    up_proj = jnp.dot(slot_rows, weight_three, preferred_element_type=jnp.float32)
    activation, silu_slope = silu_parts(gate_pre)
    hidden = (activation * up_proj).astype(jnp.bfloat16)
    return jnp.dot(hidden, weight_two, preferred_element_type=jnp.float32).astype(jnp.bfloat16)


def expert_backward(slot_rows, slot_grads, weight_one, weight_three, weight_two):
    gate_pre = jnp.dot(slot_rows, weight_one, preferred_element_type=jnp.float32)
    up_proj = jnp.dot(slot_rows, weight_three, preferred_element_type=jnp.float32)
    activation, silu_slope = silu_parts(gate_pre)
    grad_hidden = jnp.dot(slot_grads, weight_two.T, preferred_element_type=jnp.float32)
    grad_gate = (grad_hidden * up_proj * silu_slope).astype(jnp.bfloat16)
    grad_up = (grad_hidden * activation).astype(jnp.bfloat16)
    summed = jnp.dot(grad_gate, weight_one.T, preferred_element_type=jnp.float32)
    summed = summed + jnp.dot(grad_up, weight_three.T, preferred_element_type=jnp.float32)
    return summed.astype(jnp.bfloat16)


def block_grads(block_item, attn_scale):
    query_blk, key_blk, value_blk, cot_blk, state_start, state_after = block_item
    length = query_blk.shape[0]
    causal = jnp.arange(length)[:, None] >= jnp.arange(length)[None, :]
    scores = jnp.where(causal, jnp.dot(query_blk, key_blk.T, preferred_element_type=jnp.float32), 0.0).astype(jnp.bfloat16)
    probes = jnp.where(causal, jnp.dot(cot_blk, value_blk.T, preferred_element_type=jnp.float32), 0.0).astype(jnp.bfloat16)
    start_low = state_start.astype(jnp.bfloat16)
    after_low = state_after.astype(jnp.bfloat16)
    grad_query = attn_scale * (jnp.dot(probes, key_blk, preferred_element_type=jnp.float32)
                               + jnp.dot(cot_blk, start_low.T, preferred_element_type=jnp.float32))
    grad_key = attn_scale * (jnp.dot(probes.T, query_blk, preferred_element_type=jnp.float32)
                             + jnp.dot(value_blk, after_low.T, preferred_element_type=jnp.float32))
    grad_value = attn_scale * (jnp.dot(scores.T, cot_blk, preferred_element_type=jnp.float32)
                               + jnp.dot(key_blk, after_low, preferred_element_type=jnp.float32))
    return grad_query.astype(jnp.bfloat16), grad_key.astype(jnp.bfloat16), grad_value.astype(jnp.bfloat16)


def head_gradients(query_head, key_head, value_head, cot_head, attn_scale):
    total = query_head.shape[0]
    nblocks = total // BLOCK
    part_width = min(HEAD_DIM, D // N_EXP)
    query_blocks = query_head.reshape(nblocks, BLOCK, HEAD_DIM)
    key_blocks = key_head.reshape(nblocks, BLOCK, HEAD_DIM)
    sum_query = jnp.zeros((total, HEAD_DIM), jnp.float32)
    sum_key = jnp.zeros((total, HEAD_DIM), jnp.float32)
    value_parts = []
    for part_index in range(HEAD_DIM // part_width):
        low_col = part_index * part_width
        value_blocks = value_head[:, low_col:low_col + part_width].reshape(nblocks, BLOCK, part_width)
        cot_blocks = cot_head[:, low_col:low_col + part_width].reshape(nblocks, BLOCK, part_width)
        state_blocks = jnp.einsum('nbd,nbv->ndv', key_blocks.astype(jnp.float32), value_blocks.astype(jnp.float32))
        after_blocks = jnp.einsum('nbd,nbv->ndv', query_blocks.astype(jnp.float32), cot_blocks.astype(jnp.float32))
        state_start = jnp.cumsum(state_blocks, axis=0) - state_blocks
        state_after = jnp.sum(after_blocks, axis=0)[None] - jnp.cumsum(after_blocks, axis=0)

        def run_block(block_item):
            return block_grads(block_item, attn_scale)

        part_query, part_key, part_value = lax.map(
            run_block, (query_blocks, key_blocks, value_blocks, cot_blocks, state_start, state_after))
        sum_query = sum_query + part_query.reshape(total, HEAD_DIM).astype(jnp.float32)
        sum_key = sum_key + part_key.reshape(total, HEAD_DIM).astype(jnp.float32)
        value_parts.append(part_value.reshape(total, part_width))
    return sum_query.astype(jnp.bfloat16), sum_key.astype(jnp.bfloat16), jnp.concatenate(value_parts, axis=1)


def reference(tokens, expert_ids, gate_weights, weight_gate, weight_up, weight_down, attn_queries, attn_keys, grad_out):
    total = tokens.shape[0]
    model_width = tokens.shape[1]
    flat_ids = expert_ids.reshape(-1).astype(jnp.int32)
    slot_count = flat_ids.shape[0]
    cap_all = N_CTX * N_EXP * CAP
    one_hot = (flat_ids[:, None] == jnp.arange(EXPERTS, dtype=jnp.int32)[None, :]).astype(jnp.int32)
    slot_rank = jnp.sum((jnp.cumsum(one_hot, axis=0, dtype=jnp.int32) - one_hot) * one_hot, axis=1).astype(jnp.int32)
    slot_dest = (flat_ids * cap_all + slot_rank).astype(jnp.int32)
    slot_owner = (jnp.arange(slot_count, dtype=jnp.int32) // TOPK).astype(jnp.int32)
    slot_source = jnp.full((EXPERTS * cap_all,), total, jnp.int32).at[slot_dest].set(slot_owner)
    slot_gate = jnp.zeros((EXPERTS * cap_all,), jnp.float32).at[slot_dest].set(gate_weights.reshape(-1))
    slot_source = slot_source.reshape(EXPERTS, cap_all)
    slot_gate = slot_gate.reshape(EXPERTS, cap_all)
    padded = jnp.concatenate([tokens, jnp.zeros((1, model_width), jnp.bfloat16)], axis=0)

    def forward_expert(running, expert_item):
        source_ids, gate_row, weight_one, weight_three, weight_two = expert_item
        produced = expert_forward(padded[source_ids], weight_one, weight_three, weight_two)
        running = running.at[source_ids].add(gate_row[:, None] * produced.astype(jnp.float32))
        return running, None

    mixed_sum, unused = lax.scan(forward_expert, jnp.zeros((total + 1, model_width), jnp.float32),
                                 (slot_source, slot_gate, weight_gate, weight_up, weight_down))
    values = mixed_sum[:total].astype(jnp.bfloat16)

    attn_scale = 1.0 / (HEAD_DIM * TOKENS) ** 0.5

    def one_head(head_index):
        start = (head_index * HEAD_DIM).astype(jnp.int32)

        def column_slice(array):
            return lax.dynamic_slice_in_dim(array, start, HEAD_DIM, 1)

        return head_gradients(column_slice(attn_queries), column_slice(attn_keys), column_slice(values),
                              column_slice(grad_out), attn_scale)

    heads_query, heads_key, heads_value = lax.map(one_head, jnp.arange(D // HEAD_DIM, dtype=jnp.int32))

    def to_columns(stacked):
        return jnp.transpose(stacked, (1, 0, 2)).reshape(total, model_width)

    grad_queries = to_columns(heads_query)
    grad_keys = to_columns(heads_key)
    grad_values = to_columns(heads_value)
    padded_grads = jnp.concatenate([grad_values, jnp.zeros((1, model_width), jnp.bfloat16)], axis=0)

    def backward_expert(running, expert_item):
        source_ids, gate_row, weight_one, weight_three, weight_two = expert_item
        produced = expert_backward(padded[source_ids], padded_grads[source_ids], weight_one, weight_three, weight_two)
        running = running.at[source_ids].add(gate_row[:, None] * produced.astype(jnp.float32))
        return running, None

    grad_sum, unused = lax.scan(backward_expert, jnp.zeros((total + 1, model_width), jnp.float32),
                                (slot_source, slot_gate, weight_gate, weight_up, weight_down))
    grad_tokens = grad_sum[:total].astype(jnp.bfloat16)
    return grad_tokens, grad_queries, grad_keys
```

```python
import math

import jax
import jax.numpy as jnp
from jax import lax
from jax.sharding import PartitionSpec as P

HEAD_DIM = 128
TOPK = 1
BLOCK = 512


def silu_parts(gate_pre):
    sigmoid = jax.nn.sigmoid(gate_pre)
    activation = gate_pre * sigmoid
    silu_slope = sigmoid * (1.0 + gate_pre * (1.0 - sigmoid))
    return (activation, silu_slope)


def dot(left, right):
    return jnp.dot(left, right, preferred_element_type=jnp.float32)


def contract_rows(left, right):
    return lax.dot_general(
        left, right, (((1,), (1,)), ((), ())), preferred_element_type=jnp.float32
    )


def contract_first(left, right):
    return lax.dot_general(
        left, right, (((0,), (0,)), ((), ())), preferred_element_type=jnp.float32
    )


def move(buffer, axes):
    return lax.all_to_all(buffer, axes, split_axis=0, concat_axis=0, tiled=True)


def swap(block, axis, distance):
    count = lax.axis_size(axis)
    return lax.ppermute(block, axis, [(i, i ^ distance) for i in range(count)])


def pick(blocks, index):
    return lax.dynamic_index_in_dim(blocks, index, 0, keepdims=False)


def reduce_to_owner(blocks, axis):
    count = lax.axis_size(axis)
    me = lax.axis_index(axis)
    held = {offset: pick(blocks, me ^ offset) for offset in range(count)}
    distance = 1
    while distance < count:
        sent = sorted((o for o in held if o & distance), reverse=True)
        arrived = {o ^ distance: swap(held[o].astype(jnp.bfloat16), axis, distance) for o in sent}
        held = {o: held[o] + arrived[o].astype(jnp.float32) for o in held if not o & distance}
        distance *= 2
    return held[0]


def gather_by_offset(block, axis):
    count = lax.axis_size(axis)
    held = {0: block}
    distance = count // 2
    while distance:
        held.update({o | distance: swap(b, axis, distance) for o, b in list(held.items())})
        distance //= 2
    return held


def shards(
    tokens,
    expert_ids,
    gate_weights,
    weight_gate,
    weight_up,
    weight_down,
    attn_queries,
    attn_keys,
    grad_out,
):
    exp_count = lax.axis_size("exp")
    ctx_count = lax.axis_size("ctx")
    row_count, model_width = tokens.shape
    hidden_width = weight_gate.shape[2]
    slice_width = weight_gate.shape[1]
    experts = weight_gate.shape[0] * exp_count
    capacity = 5 * row_count * TOPK // (4 * exp_count)
    slots = experts * capacity
    part_width = model_width // exp_count
    key_width = max(part_width, HEAD_DIM)
    group_size = key_width // part_width
    local_heads = key_width // HEAD_DIM
    value_width = part_width // local_heads
    span_rows = row_count * exp_count
    nblocks = span_rows // BLOCK
    attn_scale = 1.0 / math.sqrt(HEAD_DIM * span_rows * ctx_count)

    weight_two = lax.all_gather(weight_down[0], "ctx", axis=1, tiled=True)

    flat_ids = expert_ids.reshape(-1)
    one_hot = flat_ids[:, None] == jnp.arange(experts, dtype=jnp.int32)[None, :]
    row_ids = jnp.arange(row_count, dtype=jnp.int32)
    before = (row_ids[None, :] < row_ids[:, None]).astype(jnp.bfloat16)
    counts = dot(before, one_hot.astype(jnp.bfloat16))
    slot_rank = jnp.sum(jnp.where(one_hot, counts, 0.0), axis=1).astype(jnp.int32)
    slot_dest = flat_ids * capacity + slot_rank
    dispatch = (jnp.arange(slots, dtype=jnp.int32)[:, None] == slot_dest[None, :]).astype(jnp.bfloat16)
    slot_rows = dot(dispatch, tokens).astype(jnp.bfloat16)
    outgoing = jnp.transpose(
        slot_rows.reshape(experts, capacity, ctx_count, slice_width), (2, 0, 1, 3)
    ).reshape(ctx_count * experts, capacity, slice_width)
    incoming = move(outgoing, ("ctx", "exp")).reshape(ctx_count * slots, slice_width)

    me = lax.axis_index("exp")
    place = flat_ids * slots + me * capacity + slot_rank
    info = jnp.concatenate(
        [place.astype(jnp.float32)[None], gate_weights.reshape(1, -1), jnp.zeros((6, row_count), jnp.float32)]
    )
    info = move(jnp.broadcast_to(info[None], (exp_count, 8, row_count)), "exp")
    span_place = info[:, 0].reshape(span_rows).astype(jnp.int32)
    span_gate = info[:, 1].reshape(span_rows, 1)
    spread = (
        span_place[:, None] == jnp.arange(experts * slots, dtype=jnp.int32)[None, :]
    ).astype(jnp.bfloat16)

    def heads_in(array):
        copies = jnp.repeat(
            jnp.transpose(array.reshape(row_count, model_width // key_width, key_width), (1, 0, 2)),
            group_size,
            axis=0,
        )
        return move(copies, "exp").reshape(span_rows, key_width)

    def to_blocks(flat, width):
        return jnp.transpose(flat.reshape(nblocks, BLOCK, local_heads, width), (0, 2, 1, 3))

    def from_blocks(blocked):
        return jnp.transpose(blocked, (0, 2, 1, 3)).reshape(span_rows, -1)

    query_blocks = to_blocks(heads_in(attn_queries), HEAD_DIM)
    key_blocks = to_blocks(heads_in(attn_keys), HEAD_DIM)
    cot_blocks = to_blocks(grad_out, value_width)

    partial = jnp.concatenate(
        [dot(incoming, weight_gate[0]), dot(incoming, weight_up[0])], axis=1
    )
    projected = reduce_to_owner(partial.reshape(ctx_count, slots, 2 * hidden_width), "ctx")
    gate_pre, up_proj = projected[:, :hidden_width], projected[:, hidden_width:]
    activation, silu_slope = silu_parts(gate_pre)

    causal = jnp.arange(BLOCK)[:, None] >= jnp.arange(BLOCK)[None, :]
    after_blocks = jnp.einsum(
        "nhbd,nhbv->nhdv", query_blocks, cot_blocks, preferred_element_type=jnp.float32
    )
    after_local = jnp.sum(after_blocks, axis=0)
    state_after = after_local[None] - jnp.cumsum(after_blocks, axis=0)
    for step in range(1, ctx_count):
        state_after = state_after + lax.ppermute(
            after_local, "ctx", [(i + step, i) for i in range(ctx_count - step)]
        )
    after_low = state_after.astype(jnp.bfloat16)
    scores = jnp.where(
        causal,
        jnp.einsum("nhtd,nhsd->nhts", query_blocks, key_blocks, preferred_element_type=jnp.float32),
        0.0,
    ).astype(jnp.bfloat16)
    grad_values = (
        attn_scale
        * (
            jnp.einsum("nhts,nhtv->nhsv", scores, cot_blocks, preferred_element_type=jnp.float32)
            + jnp.einsum("nhsd,nhdv->nhsv", key_blocks, after_low, preferred_element_type=jnp.float32)
        )
    ).astype(jnp.bfloat16)
    slot_grads = contract_first(spread, from_blocks(grad_values)).astype(jnp.bfloat16)
    slot_grads = move(slot_grads.reshape(exp_count, slots, part_width), "exp")
    slot_grads = jnp.transpose(slot_grads, (1, 0, 2)).reshape(slots, model_width)

    hidden = (activation * up_proj).astype(jnp.bfloat16)
    expert_out = dot(hidden, weight_two).astype(jnp.bfloat16)
    returned = move(
        jnp.transpose(expert_out.reshape(slots, exp_count, part_width), (1, 0, 2)), "exp"
    ).reshape(experts * slots, part_width)
    values = (span_gate * dot(spread, returned)).astype(jnp.bfloat16)

    grad_hidden = contract_rows(slot_grads, weight_two)
    grad_both = jnp.concatenate(
        [grad_hidden * up_proj * silu_slope, grad_hidden * activation], axis=1
    ).astype(jnp.bfloat16)
    home = jnp.zeros((ctx_count, slots, slice_width), jnp.bfloat16)
    for offset, block in gather_by_offset(grad_both, "ctx").items():
        expert_grad = (
            contract_rows(block[:, :hidden_width], weight_gate[0])
            + contract_rows(block[:, hidden_width:], weight_up[0])
        ).astype(jnp.bfloat16)
        home = lax.dynamic_update_index_in_dim(home, expert_grad, lax.axis_index("ctx") ^ offset, 0)
    home = move(home.reshape(ctx_count * experts, capacity, slice_width), ("ctx", "exp"))
    home = jnp.transpose(home.reshape(ctx_count, slots, slice_width), (1, 0, 2)).reshape(slots, model_width)
    grad_tokens = (gate_weights * contract_first(dispatch, home)).astype(jnp.bfloat16)

    value_blocks = to_blocks(values, value_width)
    state_blocks = jnp.einsum(
        "nhbd,nhbv->nhdv", key_blocks, value_blocks, preferred_element_type=jnp.float32
    )
    state_local = jnp.sum(state_blocks, axis=0)
    state_start = jnp.cumsum(state_blocks, axis=0) - state_blocks
    for step in range(1, ctx_count):
        state_start = state_start + lax.ppermute(
            state_local, "ctx", [(i, i + step) for i in range(ctx_count - step)]
        )
    start_low = state_start.astype(jnp.bfloat16)
    probes = jnp.where(
        causal,
        jnp.einsum("nhtv,nhsv->nhts", cot_blocks, value_blocks, preferred_element_type=jnp.float32),
        0.0,
    ).astype(jnp.bfloat16)
    part_query = attn_scale * (
        jnp.einsum("nhts,nhsd->nhtd", probes, key_blocks, preferred_element_type=jnp.float32)
        + jnp.einsum("nhtv,nhdv->nhtd", cot_blocks, start_low, preferred_element_type=jnp.float32)
    )
    part_key = attn_scale * (
        jnp.einsum("nhts,nhtd->nhsd", probes, query_blocks, preferred_element_type=jnp.float32)
        + jnp.einsum("nhsv,nhdv->nhsd", value_blocks, after_low, preferred_element_type=jnp.float32)
    )

    def heads_out(part):
        back = move(
            from_blocks(part.astype(jnp.bfloat16)).reshape(exp_count, row_count, key_width), "exp"
        )
        if group_size > 1:
            back = jnp.sum(
                back.reshape(exp_count // group_size, group_size, row_count, key_width).astype(jnp.float32),
                axis=1,
            ).astype(jnp.bfloat16)
        return jnp.transpose(back, (1, 0, 2)).reshape(row_count, model_width)

    return (grad_tokens, heads_out(part_query), heads_out(part_key))


def solution(mesh):
    in_specs = (
        P(("ctx", "exp"), None),
        P(("ctx", "exp"), None),
        P(("ctx", "exp"), None),
        P("exp", "ctx", None),
        P("exp", "ctx", None),
        P("exp", None, "ctx"),
        P(("ctx", "exp"), None),
        P(("ctx", "exp"), None),
        P("ctx", "exp"),
    )
    out_specs = (P(("ctx", "exp"), None), P(("ctx", "exp"), None), P(("ctx", "exp"), None))
    return jax.shard_map(shards, mesh=mesh, in_specs=in_specs, out_specs=out_specs, check_vma=False)
```

```python
import functools
import math

import jax
import jax.numpy as jnp
from jax import lax
from jax.experimental import pallas as pl
from jax.experimental.pallas import tpu as pltpu
from jax.sharding import Mesh
from jax.sharding import PartitionSpec as P

HEAD_DIM = 128
TOPK = 1
BLOCK = 512
VMEM_LIMIT = 32 * 1024 * 1024
BF16 = jnp.bfloat16
F32 = jnp.float32


def dot(left, right):
    return jnp.dot(left, right, preferred_element_type=F32)


def dot_nt(left, right):
    return lax.dot_general(left, right, (((1,), (1,)), ((), ())), preferred_element_type=F32)


def dot_tn(left, right):
    return lax.dot_general(left, right, (((0,), (0,)), ((), ())), preferred_element_type=F32)


def iota(shape, axis):
    return lax.broadcasted_iota(jnp.int32, shape, axis)


def run(kernel, outs, args, scratch=(), us=1):
    in_specs = [
        pl.BlockSpec(memory_space=pltpu.SMEM if a.dtype == jnp.int32 and a.ndim == 1 else pltpu.VMEM)
        for a in args
    ]
    moved = sum(math.prod(a.shape) * a.dtype.itemsize for a in (*args, *outs))
    return pl.pallas_call(
        kernel,
        out_shape=tuple(outs),
        in_specs=in_specs,
        out_specs=tuple(pl.BlockSpec(memory_space=pltpu.VMEM) for _ in outs),
        scratch_shapes=list(scratch),
        compiler_params=pltpu.CompilerParams(vmem_limit_bytes=VMEM_LIMIT),
        cost_estimate=pl.CostEstimate(flops=int(us * 1.15e9), bytes_accessed=moved // 100, transcendentals=0),
    )(*args)


def shape(dims, dtype):
    return jax.ShapeDtypeStruct(dims, dtype)


def row_slots(ids, pad, wide):
    rows = ids.shape[0]
    named = ids == iota((rows, 128 * -(-wide // 128)), 1)
    earlier = (iota((rows, rows), 1) < iota((rows, rows), 0)).astype(BF16)
    counts = dot(earlier, named.astype(BF16))
    rank = jnp.sum(jnp.where(named, counts, 0.0), axis=1, keepdims=True).astype(jnp.int32)
    chosen = (ids * pad + rank == iota((rows, wide * pad), 1)).astype(BF16)
    return rank, chosen


def packing(experts, capacity, pad):
    slots = experts * capacity
    row, col = iota((slots, experts * pad), 0), iota((slots, experts * pad), 1)
    expert = col // pad
    inner = col - expert * pad
    return ((inner < capacity) & (row == expert * capacity + inner)).astype(BF16)


def unpacking(experts, capacity, pad):
    slots = experts * capacity
    row, col = iota((experts * pad, slots), 0), iota((experts * pad, slots), 1)
    expert = row // pad
    inner = row - expert * pad
    return ((inner < capacity) & (col == expert * capacity + inner)).astype(BF16)


FACTS = 16


def route_kernel(
    hi, exp, group, capacity, pad, ids_ref, gate_ref, tokens_ref, query_ref, key_ref, out_ref, query_out, key_out
):
    rows, width = tokens_ref.shape
    part = width // hi
    ids = ids_ref[...]
    rank, chosen = row_slots(ids, pad, exp)
    slot_rows = dot_tn(chosen, tokens_ref[...]).astype(BF16)
    for c in range(hi):
        for e in range(exp):
            out_ref[c * exp + e] = slot_rows[e * pad : e * pad + capacity, c * part : (c + 1) * part]
    gate = gate_ref[...]
    high = gate.astype(BF16).astype(F32)
    mid = (gate - high).astype(BF16).astype(F32)
    lane = iota((rows, 128), 1)
    facts = jnp.zeros((rows, 128), F32)
    for col, fact in enumerate((ids.astype(F32), rank.astype(F32), high, mid, gate - high - mid)):
        facts = jnp.where(lane == col, fact, facts)
    facts = facts.T[:FACTS].astype(BF16)
    key_width = key_out.shape[2]
    for e in range(exp):
        cols = slice(e // group * key_width, (e // group + 1) * key_width)
        query_out[e] = query_ref[:, cols]
        key_out[e, :rows] = key_ref[:, cols]
        key_out[e, rows:] = jnp.zeros((FACTS, key_width), BF16)
        key_out[e, rows:, :rows] = facts


def facts_of(key_ref, source):
    rows = key_ref.shape[1] - FACTS
    return key_ref[source, rows:, :rows].astype(F32)


def key_rows(key_ref, block, cols):
    rows = key_ref.shape[1] - FACTS
    each = BLOCK // rows
    return jnp.concatenate([key_ref[s, :rows, cols] for s in range(block * each, (block + 1) * each)], axis=0)


def slice_cols(index, width):
    return pl.ds(pl.multiple_of(index * width, 128), width)


def project_kernel(ctx, exp, capacity, pad, me_ref, in_ref, gate_ref, up_ref, *rest):
    out_refs, (padded, packed) = rest[:-2], rest[-2:]
    slots = exp * capacity
    hidden = gate_ref.shape[1]
    select = packing(exp, capacity, pad)
    padded[...] = jnp.zeros_like(padded)
    for offset in range(ctx):
        chunk = me_ref[0] ^ offset
        for e in range(exp):
            padded[e * pad : e * pad + capacity, :] = in_ref[chunk * exp + e]
        packed[offset * slots : (offset + 1) * slots, :] = dot(select, padded[...]).astype(BF16)
    for col, weight in enumerate((gate_ref, up_ref)):
        product = dot(packed[...], weight[...])
        for offset in range(ctx):
            out_refs[offset][:, col * hidden : (col + 1) * hidden] = product[
                offset * slots : (offset + 1) * slots
            ].astype(out_refs[offset].dtype)


def gates_kernel(terms, me_ref, grads_ref, *rest):
    sums, downs, (out_ref, active_ref, rows) = rest[:terms], rest[terms:-3], rest[-3:]
    hidden, depth = downs[0].shape
    parts, _, part = grads_ref.shape
    for e in range(parts):
        rows[:, e * part : (e + 1) * part] = grads_ref[e]
    projected = sums[0][...]
    for other in sums[1:]:
        projected = projected + other[...].astype(F32)
    gate, up = projected[:, :hidden], projected[:, hidden:]
    sigmoid = jax.nn.sigmoid(gate)
    active = gate * sigmoid
    active_ref[...] = (active * up).astype(BF16)
    grad = 0.0
    for o, down in enumerate(downs):
        grad += dot_nt(rows[:, slice_cols(me_ref[0] ^ o if len(downs) > 1 else 0, depth)], down[...])
    out_ref[:, :hidden] = (grad * up * (sigmoid * (1.0 + gate * (1.0 - sigmoid)))).astype(BF16)
    out_ref[:, hidden:] = (grad * active).astype(BF16)


def forward_kernel(me_ref, active_ref, *rest):
    downs, out_ref = rest[:-1], rest[-1]
    parts, _, part = out_ref.shape
    each = parts // len(downs)
    for o, down in enumerate(downs):
        product = dot(active_ref[...], down[...]).astype(BF16)
        for b in range(each):
            place = (me_ref[0] ^ o) * each + b if len(downs) > 1 else b
            out_ref[place] = product[:, b * part : (b + 1) * part]


def backward_kernel(ctx, exp, capacity, pad, me_ref, gate_ref, up_ref, *rest):
    chunks, (out_ref, grads) = rest[:-2], rest[-2:]
    hidden = gate_ref.shape[1]
    slots = exp * capacity
    for offset in range(ctx):
        grads[offset * slots : (offset + 1) * slots, :] = chunks[offset][...]
    product = (dot_nt(grads[:, :hidden], gate_ref[...]) + dot_nt(grads[:, hidden:], up_ref[...])).astype(BF16)
    spread = unpacking(exp, capacity, pad)
    for offset in range(ctx):
        chunk = me_ref[0] ^ offset
        rows = dot(spread, product[offset * slots : (offset + 1) * slots]).astype(BF16)
        for e in range(exp):
            out_ref[chunk * exp + e] = rows[e * pad : e * pad + capacity]


def home_kernel(ctx, exp, capacity, pad, ids_ref, gate_ref, in_ref, out_ref, padded):
    part = in_ref.shape[2]
    rank, chosen = row_slots(ids_ref[...], pad, exp)
    padded[...] = jnp.zeros_like(padded)
    for c in range(ctx):
        for e in range(exp):
            padded[e * pad : e * pad + capacity, c * part : (c + 1) * part] = in_ref[c * exp + e]
    out_ref[...] = (gate_ref[...] * dot(chosen, padded[...])).astype(BF16)


def row_place(ids, rank, source, capacity, slots):
    return ids * slots + source * capacity + rank


def after_kernel(heads, query_ref, cot_ref, out_ref):
    width = cot_ref.shape[1] // heads
    for h in range(heads):
        out_ref[h] = dot_tn(
            query_ref[:, h * HEAD_DIM : (h + 1) * HEAD_DIM], cot_ref[:, h * width : (h + 1) * width]
        ).astype(BF16)


def grad_values_kernel(heads, capacity, scale, query_ref, key_ref, cot_ref, *rest):
    arrived, (out_ref, low_ref, grads) = rest[:-3], rest[-3:]
    span, total = cot_ref.shape
    width = total // heads
    blocks = span // BLOCK
    causal = iota((BLOCK, BLOCK), 0) >= iota((BLOCK, BLOCK), 1)
    for h in range(heads):
        keys, cols = slice(h * HEAD_DIM, (h + 1) * HEAD_DIM), slice(h * width, (h + 1) * width)
        state = arrived[0][h].astype(F32)
        for other in arrived[1:]:
            state = state + other[h].astype(F32)
        for n in reversed(range(blocks)):
            rows = slice(n * BLOCK, (n + 1) * BLOCK)
            low = state.astype(BF16)
            low_ref[n * heads + h] = low
            query, key, cot = query_ref[rows, keys], key_rows(key_ref, n, keys), cot_ref[rows, cols]
            scores = jnp.where(causal, dot_nt(query, key), 0.0).astype(BF16)
            grads[rows, cols] = (scale * (dot_tn(scores, cot) + dot(key, low))).astype(BF16)
            if n:
                state = state + dot_tn(query, cot)
    sources, slots = key_ref.shape[0], out_ref.shape[1]
    facts = [facts_of(key_ref, s) for s in range(sources)]
    place = jnp.concatenate(
        [
            row_place(
                facts[s][0:1].astype(jnp.int32), facts[s][1:2].astype(jnp.int32), s, capacity, slots
            )
            for s in range(sources)
        ],
        axis=1,
    )
    row = iota((slots, span), 0)
    for e in range(out_ref.shape[0]):
        chosen = (place == row + e * slots).astype(BF16)
        out_ref[e] = dot(chosen, grads[...]).astype(BF16)


def grad_heads_kernel(
    heads, capacity, scale, query_ref, key_ref, cot_ref, low_ref, in_ref, key_out, part_out, state_out
):
    span, total = cot_ref.shape
    width = total // heads
    blocks = span // BLOCK
    slots = in_ref.shape[1]
    rows_each = key_ref.shape[1] - FACTS
    returned = in_ref[...].reshape(-1, total)
    causal = iota((BLOCK, BLOCK), 0) >= iota((BLOCK, BLOCK), 1)
    states = [jnp.zeros((HEAD_DIM, width), F32) for _ in range(heads)]
    for n in range(blocks):
        rows = slice(n * BLOCK, (n + 1) * BLOCK)
        places, weights = [], []
        for s in range(n * BLOCK // rows_each, (n + 1) * BLOCK // rows_each):
            facts = facts_of(key_ref, s).T
            places.append(
                row_place(
                    facts[:, 0:1].astype(jnp.int32), facts[:, 1:2].astype(jnp.int32), s, capacity, slots
                )
            )
            weights.append(facts[:, 2:3] + facts[:, 3:4] + facts[:, 4:5])
        place, weight = jnp.concatenate(places, axis=0), jnp.concatenate(weights, axis=0)
        chosen = (place == iota((BLOCK, returned.shape[0]), 1)).astype(BF16)
        values = (weight * dot(chosen, returned)).astype(BF16)
        for h in range(heads):
            keys, cols = slice(h * HEAD_DIM, (h + 1) * HEAD_DIM), slice(h * width, (h + 1) * width)
            query, key, cot = query_ref[rows, keys], key_rows(key_ref, n, keys), cot_ref[rows, cols]
            value = values[:, cols]
            probes = jnp.where(causal, dot_nt(cot, value), 0.0).astype(BF16)
            key_out[rows, keys] = (
                scale * (dot_tn(probes, query) + dot_nt(value, low_ref[n * heads + h]))
            ).astype(BF16)
            part = dot(probes, key)
            if n:
                part = part + dot_nt(cot, states[h].astype(BF16))
            part_out[rows, keys] = part
            states[h] = states[h] + dot_tn(key, value)
    for h in range(heads):
        state_out[h] = states[h].astype(BF16)


def finish_kernel(heads, scale, cot_ref, part_ref, grad_key_ref, *rest):
    arrived, out_ref = rest[:-1], rest[-1]
    width = cot_ref.shape[1] // heads
    sources, rows = out_ref.shape[0] // 2, out_ref.shape[1]
    for h in range(heads):
        keys, cols = slice(h * HEAD_DIM, (h + 1) * HEAD_DIM), slice(h * width, (h + 1) * width)
        state = arrived[0][h].astype(F32)
        for other in arrived[1:]:
            state = state + other[h].astype(F32)
        grad = (scale * (part_ref[:, keys] + dot_nt(cot_ref[:, cols], state.astype(BF16)))).astype(BF16)
        for s in range(sources):
            out_ref[2 * s, :, keys] = grad[s * rows : (s + 1) * rows]
    for s in range(sources):
        out_ref[2 * s + 1] = grad_key_ref[s * rows : (s + 1) * rows]


def heads_kernel(group, in_ref, query_ref, key_ref):
    sources, both, key_width = in_ref.shape
    rows = both // 2
    for n in range(sources // group):
        for place, out in enumerate((query_ref, key_ref)):
            inner = slice(place * rows, (place + 1) * rows)
            total = in_ref[n * group, inner]
            if group > 1:
                total = total.astype(F32)
                for part in range(1, group):
                    total = total + in_ref[n * group + part, inner].astype(F32)
            out[:, n * key_width : (n + 1) * key_width] = total.astype(BF16)


def move(buffer, axes):
    return lax.all_to_all(buffer, axes, split_axis=0, concat_axis=0, tiled=True)


CTX = ("hi", "lo")
ALL = ("hi", "lo", "exp")


def swap(block, distance):
    count = lax.axis_size("hi") * lax.axis_size("lo")
    return lax.ppermute(block, CTX, [(i, i ^ distance) for i in range(count)])


def spread_rest(chunks, distances):
    chunks = dict(chunks)
    for distance in sorted(distances, reverse=True):
        for o in [o for o in chunks if not o & distance and o and o | distance not in chunks and o > distance]:
            chunks[o | distance] = swap(chunks[o], distance)
    return chunks


def sum_own(terms):
    count, distance = len(terms), 1
    held, own = dict(enumerate(terms)), [terms[0]]
    while distance < count:
        urgent = sorted((o for o in held if o & distance and o != distance), reverse=True)
        arrived = {o ^ distance: swap(held[o].astype(BF16), distance) for o in urgent}
        last = held[distance].astype(BF16)
        held = {o: held[o].astype(F32) + term.astype(F32) for o, term in arrived.items()}
        if held:
            first = max(held)
            held[first] = held[first].astype(BF16)
        own.append(swap(last, distance))
        distance *= 2
    return own


def shards(
    tokens,
    expert_ids,
    gate_weights,
    weight_gate,
    weight_up,
    weight_down,
    attn_queries,
    attn_keys,
    grad_out,
):
    exp, hi, lo = lax.axis_size("exp"), lax.axis_size("hi"), lax.axis_size("lo")
    ctx = hi * lo
    rows, width = tokens.shape
    slice_width, hidden = weight_gate.shape[1:]
    capacity = 5 * rows * TOPK // (4 * exp)
    pad = 16 * -(-capacity // 16)
    slots = exp * capacity
    part_width = width // exp
    key_width = max(part_width, HEAD_DIM)
    group = key_width // part_width
    heads = key_width // HEAD_DIM
    span = rows * exp
    scale = 1.0 / math.sqrt(HEAD_DIM * span * ctx)
    me = lax.axis_index(CTX).astype(jnp.int32).reshape(1)
    state_low = shape((heads, HEAD_DIM, part_width // heads), BF16)

    outgoing, query, key = run(
        functools.partial(route_kernel, ctx, exp, group, capacity, pad),
        [
            shape((ctx * exp, capacity, slice_width), BF16),
            shape((exp, rows, key_width), BF16),
            shape((exp, rows + FACTS, key_width), BF16),
        ],
        [expert_ids, gate_weights, tokens, attn_queries, attn_keys],
    )
    doubling = [1 << n for n in range((ctx - 1).bit_length())]

    downs = {0: weight_down[0]}
    for distance in reversed(doubling):
        downs[distance] = swap(weight_down[0], distance)

    straight = [downs[d] for d in doubling]

    query = move(query, "exp").reshape(span, key_width)
    key, query = lax.optimization_barrier((key, query))
    (after,) = run(functools.partial(after_kernel, heads), [state_low], [query, grad_out])
    after_in = [
        lax.ppermute(after, CTX, [(i + step, i) for i in range(ctx - step)]) for step in range(1, ctx)
    ]
    key = move(key, "exp")
    outgoing, key, straight = lax.optimization_barrier((outgoing, key, straight))
    incoming = move(outgoing, ALL)
    downs = spread_rest({0: downs[0], **dict(zip(doubling, straight, strict=True))}, doubling)
    rest = [downs[o] for o in range(1, ctx) if o & (o - 1)]

    terms = run(
        functools.partial(project_kernel, ctx, exp, capacity, pad),
        [shape((slots, 2 * hidden), BF16 if o & 1 else F32) for o in range(ctx)],
        [me, incoming, weight_gate[0], weight_up[0]],
        scratch=[
            pltpu.VMEM((exp * pad, slice_width), BF16),
            pltpu.VMEM((ctx * slots, slice_width), BF16),
        ],
        us=4,
    )
    terms, rest = lax.optimization_barrier((terms, rest))
    downs.update(zip((o for o in range(1, ctx) if o & (o - 1)), rest, strict=True))
    downs = [downs[o] for o in range(ctx)]
    terms = sum_own(terms)

    grad_rows, after_low = run(
        functools.partial(grad_values_kernel, heads, capacity, scale),
        [
            shape((exp, slots, part_width), BF16),
            shape((span // BLOCK * heads, HEAD_DIM, part_width // heads), BF16),
        ],
        [query, key, grad_out, *after_in],
        scratch=[pltpu.VMEM((span, part_width), BF16)],
        us=3,
    )
    grad_rows = move(grad_rows, "exp")

    grads, active = run(
        functools.partial(gates_kernel, len(terms)),
        [shape((slots, 2 * hidden), BF16), shape((slots, hidden), BF16)],
        [me, grad_rows, *terms, *downs],
        scratch=[pltpu.VMEM((slots, width), BF16)], us=0)
    chunks = {0: grads, **{d: swap(grads, d) for d in reversed(doubling)}}
    (expert_out,) = run(
        forward_kernel,
        [shape((exp, slots, part_width), BF16)],
        [me, active, *downs], us=0)
    grad_key, query_part, state = run(
        functools.partial(grad_heads_kernel, heads, capacity, scale),
        [shape((span, key_width), BF16), shape((span, key_width), F32), state_low],
        [query, key, grad_out, after_low, move(expert_out, "exp")], us=0)
    state_in = [
        lax.ppermute(state, CTX, [(i, i + step) for i in range(ctx - step)]) for step in range(1, ctx)
    ]
    far = doubling[-1]
    chunks[far], state_in = lax.optimization_barrier((chunks[far], state_in))
    chunks = spread_rest(chunks, doubling)
    chunks = [chunks[o] for o in range(ctx)]
    (outgoing,) = run(
        functools.partial(backward_kernel, ctx, exp, capacity, pad),
        [shape((ctx * exp, capacity, slice_width), BF16)],
        [me, weight_gate[0], weight_up[0], *chunks],
        scratch=[pltpu.VMEM((ctx * slots, 2 * hidden), BF16)],
        us=60,
    )
    (heads_back,) = run(
        functools.partial(finish_kernel, heads, scale),
        [shape((2 * exp, rows, key_width), BF16)],
        [grad_out, query_part, grad_key, *state_in],
        us=0,
    )
    heads_back = move(heads_back.reshape(exp, 2 * rows, key_width), "exp")
    home = move(outgoing, ALL)
    grad_queries, grad_keys = run(
        functools.partial(heads_kernel, group), [shape((rows, width), BF16)] * 2, [heads_back]
    )
    (grad_tokens,) = run(
        functools.partial(home_kernel, ctx, exp, capacity, pad),
        [shape((rows, width), BF16)],
        [expert_ids, gate_weights, home],
        scratch=[pltpu.VMEM((exp * pad, width), BF16)],
    )
    return grad_tokens, grad_queries, grad_keys


def solution(mesh):
    ctx, exp = mesh.shape["ctx"], mesh.shape["exp"]
    lo = 2 if ctx % 2 == 0 else 1
    split = Mesh(mesh.devices.reshape(ctx // lo, lo, exp), ("hi", "lo", "exp"))
    rows, span = P(("hi", "lo", "exp"), None), ("hi", "lo")
    in_specs = (
        rows,
        rows,
        rows,
        P("exp", span, None),
        P("exp", span, None),
        P("exp", None, span),
        rows,
        rows,
        P(span, "exp"),
    )
    return jax.shard_map(
        shards, mesh=split, in_specs=in_specs, out_specs=(rows, rows, rows), check_vma=False
    )
```

```python
import functools
import math

import jax
import jax.numpy as jnp
from jax import lax
from jax.experimental import pallas as pl
from jax.experimental.pallas import tpu as pltpu
from jax.sharding import Mesh
from jax.sharding import PartitionSpec as P

HEAD_DIM = 128
TOPK = 1
BLOCK = 512
VMEM_LIMIT = 32 * 1024 * 1024
BF16 = jnp.bfloat16
F32 = jnp.float32


def dot(left, right):
    return jnp.dot(left, right, preferred_element_type=F32)


def dot_nt(left, right):
    return lax.dot_general(left, right, (((1,), (1,)), ((), ())), preferred_element_type=F32)


def dot_tn(left, right):
    return lax.dot_general(left, right, (((0,), (0,)), ((), ())), preferred_element_type=F32)


def iota(shape, axis):
    return lax.broadcasted_iota(jnp.int32, shape, axis)


def run(kernel, outs, args, scratch=(), us=1):
    in_specs = [
        pl.BlockSpec(memory_space=pltpu.SMEM if a.dtype == jnp.int32 and a.ndim == 1 else pltpu.VMEM)
        for a in args
    ]
    moved = sum(math.prod(a.shape) * a.dtype.itemsize for a in (*args, *outs))
    return pl.pallas_call(
        kernel,
        out_shape=tuple(outs),
        in_specs=in_specs,
        out_specs=tuple(pl.BlockSpec(memory_space=pltpu.VMEM) for _ in outs),
        scratch_shapes=list(scratch),
        compiler_params=pltpu.CompilerParams(vmem_limit_bytes=VMEM_LIMIT),
        cost_estimate=pl.CostEstimate(flops=int(us * 1.15e9), bytes_accessed=moved // 100, transcendentals=0),
    )(*args)


def shape(dims, dtype):
    return jax.ShapeDtypeStruct(dims, dtype)


def row_slots(ids, pad, wide):
    rows = ids.shape[0]
    named = ids == iota((rows, 128 * -(-wide // 128)), 1)
    earlier = (iota((rows, rows), 1) < iota((rows, rows), 0)).astype(BF16)
    counts = dot(earlier, named.astype(BF16))
    rank = jnp.sum(jnp.where(named, counts, 0.0), axis=1, keepdims=True).astype(jnp.int32)
    chosen = (ids * pad + rank == iota((rows, wide * pad), 1)).astype(BF16)
    return rank, chosen


def packing(experts, capacity, pad):
    slots = experts * capacity
    row, col = iota((slots, experts * pad), 0), iota((slots, experts * pad), 1)
    expert = col // pad
    inner = col - expert * pad
    return ((inner < capacity) & (row == expert * capacity + inner)).astype(BF16)


def unpacking(experts, capacity, pad):
    slots = experts * capacity
    row, col = iota((experts * pad, slots), 0), iota((experts * pad, slots), 1)
    expert = row // pad
    inner = row - expert * pad
    return ((inner < capacity) & (col == expert * capacity + inner)).astype(BF16)


FACTS = 16


def route_kernel(
    hi, exp, group, capacity, pad, ids_ref, gate_ref, tokens_ref, query_ref, key_ref, out_ref, query_out, key_out
):
    rows, width = tokens_ref.shape
    part = width // hi
    ids = ids_ref[...]
    rank, chosen = row_slots(ids, pad, exp)
    slot_rows = dot_tn(chosen, tokens_ref[...]).astype(BF16)
    for c in range(hi):
        for e in range(exp):
            out_ref[c * exp + e] = slot_rows[e * pad : e * pad + capacity, c * part : (c + 1) * part]
    gate = gate_ref[...]
    high = gate.astype(BF16).astype(F32)
    mid = (gate - high).astype(BF16).astype(F32)
    lane = iota((rows, 128), 1)
    facts = jnp.zeros((rows, 128), F32)
    for col, fact in enumerate((ids.astype(F32), rank.astype(F32), high, mid, gate - high - mid)):
        facts = jnp.where(lane == col, fact, facts)
    facts = facts.T[:FACTS].astype(BF16)
    key_width = key_out.shape[2]
    for e in range(exp):
        cols = slice(e // group * key_width, (e // group + 1) * key_width)
        query_out[e] = query_ref[:, cols]
        key_out[e, :rows] = key_ref[:, cols]
        key_out[e, rows:] = jnp.zeros((FACTS, key_width), BF16)
        key_out[e, rows:, :rows] = facts


def facts_of(key_ref, source):
    rows = key_ref.shape[1] - FACTS
    return key_ref[source, rows:, :rows].astype(F32)


def key_rows(key_ref, block, cols):
    rows = key_ref.shape[1] - FACTS
    each = BLOCK // rows
    return jnp.concatenate([key_ref[s, :rows, cols] for s in range(block * each, (block + 1) * each)], axis=0)


def slice_cols(index, width):
    return pl.ds(pl.multiple_of(index * width, 128), width)


def project_kernel(ctx, exp, capacity, pad, me_ref, in_ref, gate_ref, up_ref, *rest):
    out_refs, (padded, packed) = rest[:-2], rest[-2:]
    slots = exp * capacity
    hidden = gate_ref.shape[1]
    select = packing(exp, capacity, pad)
    padded[...] = jnp.zeros_like(padded)
    for offset in range(ctx):
        chunk = me_ref[0] ^ offset
        for e in range(exp):
            padded[e * pad : e * pad + capacity, :] = in_ref[chunk * exp + e]
        packed[offset * slots : (offset + 1) * slots, :] = dot(select, padded[...]).astype(BF16)
    for col, weight in enumerate((gate_ref, up_ref)):
        product = dot(packed[...], weight[...])
        for offset in range(ctx):
            out_refs[offset][:, col * hidden : (col + 1) * hidden] = product[
                offset * slots : (offset + 1) * slots
            ].astype(out_refs[offset].dtype)


def gates_kernel(terms, me_ref, grads_ref, *rest):
    sums, downs, (out_ref, active_ref, rows) = rest[:terms], rest[terms:-3], rest[-3:]
    hidden, depth = downs[0].shape
    parts, _, part = grads_ref.shape
    for e in range(parts):
        rows[:, e * part : (e + 1) * part] = grads_ref[e]
    projected = sums[0][...]
    for other in sums[1:]:
        projected = projected + other[...].astype(F32)
    gate, up = projected[:, :hidden], projected[:, hidden:]
    sigmoid = jax.nn.sigmoid(gate)
    active = gate * sigmoid
    active_ref[...] = (active * up).astype(BF16)
    grad = 0.0
    for o, down in enumerate(downs):
        grad += dot_nt(rows[:, slice_cols(me_ref[0] ^ o if len(downs) > 1 else 0, depth)], down[...])
    out_ref[:, :hidden] = (grad * up * (sigmoid * (1.0 + gate * (1.0 - sigmoid)))).astype(BF16)
    out_ref[:, hidden:] = (grad * active).astype(BF16)


def forward_kernel(me_ref, active_ref, *rest):
    downs, out_ref = rest[:-1], rest[-1]
    parts, _, part = out_ref.shape
    each = parts // len(downs)
    for o, down in enumerate(downs):
        product = dot(active_ref[...], down[...]).astype(BF16)
        for b in range(each):
            place = (me_ref[0] ^ o) * each + b if len(downs) > 1 else b
            out_ref[place] = product[:, b * part : (b + 1) * part]


def backward_kernel(ctx, exp, capacity, pad, me_ref, gate_ref, up_ref, *rest):
    chunks, (out_ref, grads) = rest[:-2], rest[-2:]
    hidden = gate_ref.shape[1]
    slots = exp * capacity
    for offset in range(ctx):
        grads[offset * slots : (offset + 1) * slots, :] = chunks[offset][...]
    product = (dot_nt(grads[:, :hidden], gate_ref[...]) + dot_nt(grads[:, hidden:], up_ref[...])).astype(BF16)
    spread = unpacking(exp, capacity, pad)
    for offset in range(ctx):
        chunk = me_ref[0] ^ offset
        rows = dot(spread, product[offset * slots : (offset + 1) * slots]).astype(BF16)
        for e in range(exp):
            out_ref[chunk * exp + e] = rows[e * pad : e * pad + capacity]


def home_kernel(ctx, exp, capacity, pad, ids_ref, gate_ref, in_ref, out_ref, padded):
    part = in_ref.shape[2]
    rank, chosen = row_slots(ids_ref[...], pad, exp)
    padded[...] = jnp.zeros_like(padded)
    for c in range(ctx):
        for e in range(exp):
            padded[e * pad : e * pad + capacity, c * part : (c + 1) * part] = in_ref[c * exp + e]
    out_ref[...] = (gate_ref[...] * dot(chosen, padded[...])).astype(BF16)


def row_place(ids, rank, source, capacity, slots):
    return ids * slots + source * capacity + rank


def after_kernel(heads, query_ref, cot_ref, out_ref):
    width = cot_ref.shape[1] // heads
    for h in range(heads):
        out_ref[h] = dot_tn(
            query_ref[:, h * HEAD_DIM : (h + 1) * HEAD_DIM], cot_ref[:, h * width : (h + 1) * width]
        ).astype(BF16)


def grad_values_kernel(heads, capacity, scale, query_ref, key_ref, cot_ref, *rest):
    arrived, (out_ref, low_ref, grads) = rest[:-3], rest[-3:]
    span, total = cot_ref.shape
    width = total // heads
    blocks = span // BLOCK
    causal = iota((BLOCK, BLOCK), 0) >= iota((BLOCK, BLOCK), 1)
    for h in range(heads):
        keys, cols = slice(h * HEAD_DIM, (h + 1) * HEAD_DIM), slice(h * width, (h + 1) * width)
        state = arrived[0][h].astype(F32)
        for other in arrived[1:]:
            state = state + other[h].astype(F32)
        for n in reversed(range(blocks)):
            rows = slice(n * BLOCK, (n + 1) * BLOCK)
            low = state.astype(BF16)
            low_ref[n * heads + h] = low
            query, key, cot = query_ref[rows, keys], key_rows(key_ref, n, keys), cot_ref[rows, cols]
            scores = jnp.where(causal, dot_nt(query, key), 0.0).astype(BF16)
            grads[rows, cols] = (scale * (dot_tn(scores, cot) + dot(key, low))).astype(BF16)
            if n:
                state = state + dot_tn(query, cot)
    sources, slots = key_ref.shape[0], out_ref.shape[1]
    facts = [facts_of(key_ref, s) for s in range(sources)]
    place = jnp.concatenate(
        [
            row_place(
                facts[s][0:1].astype(jnp.int32), facts[s][1:2].astype(jnp.int32), s, capacity, slots
            )
            for s in range(sources)
        ],
        axis=1,
    )
    row = iota((slots, span), 0)
    for e in range(out_ref.shape[0]):
        chosen = (place == row + e * slots).astype(BF16)
        out_ref[e] = dot(chosen, grads[...]).astype(BF16)


def grad_heads_kernel(
    heads, capacity, scale, query_ref, key_ref, cot_ref, low_ref, in_ref, key_out, part_out, state_out
):
    span, total = cot_ref.shape
    width = total // heads
    blocks = span // BLOCK
    slots = in_ref.shape[1]
    rows_each = key_ref.shape[1] - FACTS
    returned = in_ref[...].reshape(-1, total)
    causal = iota((BLOCK, BLOCK), 0) >= iota((BLOCK, BLOCK), 1)
    states = [jnp.zeros((HEAD_DIM, width), F32) for _ in range(heads)]
    for n in range(blocks):
        rows = slice(n * BLOCK, (n + 1) * BLOCK)
        places, weights = [], []
        for s in range(n * BLOCK // rows_each, (n + 1) * BLOCK // rows_each):
            facts = facts_of(key_ref, s).T
            places.append(
                row_place(
                    facts[:, 0:1].astype(jnp.int32), facts[:, 1:2].astype(jnp.int32), s, capacity, slots
                )
            )
            weights.append(facts[:, 2:3] + facts[:, 3:4] + facts[:, 4:5])
        place, weight = jnp.concatenate(places, axis=0), jnp.concatenate(weights, axis=0)
        chosen = (place == iota((BLOCK, returned.shape[0]), 1)).astype(BF16)
        values = (weight * dot(chosen, returned)).astype(BF16)
        for h in range(heads):
            keys, cols = slice(h * HEAD_DIM, (h + 1) * HEAD_DIM), slice(h * width, (h + 1) * width)
            query, key, cot = query_ref[rows, keys], key_rows(key_ref, n, keys), cot_ref[rows, cols]
            value = values[:, cols]
            probes = jnp.where(causal, dot_nt(cot, value), 0.0).astype(BF16)
            key_out[rows, keys] = (
                scale * (dot_tn(probes, query) + dot_nt(value, low_ref[n * heads + h]))
            ).astype(BF16)
            part = dot(probes, key)
            if n:
                part = part + dot_nt(cot, states[h].astype(BF16))
            part_out[rows, keys] = part
            states[h] = states[h] + dot_tn(key, value)
    for h in range(heads):
        state_out[h] = states[h].astype(BF16)


def finish_kernel(heads, scale, cot_ref, part_ref, grad_key_ref, *rest):
    arrived, out_ref = rest[:-1], rest[-1]
    width = cot_ref.shape[1] // heads
    sources, rows = out_ref.shape[0] // 2, out_ref.shape[1]
    for h in range(heads):
        keys, cols = slice(h * HEAD_DIM, (h + 1) * HEAD_DIM), slice(h * width, (h + 1) * width)
        state = arrived[0][h].astype(F32)
        for other in arrived[1:]:
            state = state + other[h].astype(F32)
        grad = (scale * (part_ref[:, keys] + dot_nt(cot_ref[:, cols], state.astype(BF16)))).astype(BF16)
        for s in range(sources):
            out_ref[2 * s, :, keys] = grad[s * rows : (s + 1) * rows]
    for s in range(sources):
        out_ref[2 * s + 1] = grad_key_ref[s * rows : (s + 1) * rows]


def heads_kernel(group, in_ref, query_ref, key_ref):
    sources, both, key_width = in_ref.shape
    rows = both // 2
    for n in range(sources // group):
        for place, out in enumerate((query_ref, key_ref)):
            inner = slice(place * rows, (place + 1) * rows)
            total = in_ref[n * group, inner]
            if group > 1:
                total = total.astype(F32)
                for part in range(1, group):
                    total = total + in_ref[n * group + part, inner].astype(F32)
            out[:, n * key_width : (n + 1) * key_width] = total.astype(BF16)


def move(buffer, axes):
    return lax.all_to_all(buffer, axes, split_axis=0, concat_axis=0, tiled=True)


CTX = ("hi", "lo")
ALL = ("hi", "lo", "exp")


def swap(block, distance):
    count = lax.axis_size("hi") * lax.axis_size("lo")
    return lax.ppermute(block, CTX, [(i, i ^ distance) for i in range(count)])


def spread_rest(chunks, distances):
    chunks = dict(chunks)
    for distance in sorted(distances, reverse=True):
        for o in [o for o in chunks if not o & distance and o and o | distance not in chunks and o > distance]:
            chunks[o | distance] = swap(chunks[o], distance)
    return chunks


def sum_own(terms, rest):
    count, distance = len(terms), 1
    held, own = dict(enumerate(terms)), [terms[0]]
    while distance < count:
        urgent = sorted((o for o in held if o & distance and o != distance), reverse=True)
        arrived = {o ^ distance: swap(held[o].astype(BF16), distance) for o in urgent}
        last = held[distance].astype(BF16)
        held = {o: held[o].astype(F32) + term.astype(F32) for o, term in arrived.items()}
        if distance == 1:
            last, rest = lax.optimization_barrier((last, rest))
        own.append(swap(last, distance))
        distance *= 2
    return own, rest


def shards(
    tokens,
    expert_ids,
    gate_weights,
    weight_gate,
    weight_up,
    weight_down,
    attn_queries,
    attn_keys,
    grad_out,
):
    exp, hi, lo = lax.axis_size("exp"), lax.axis_size("hi"), lax.axis_size("lo")
    ctx = hi * lo
    rows, width = tokens.shape
    slice_width, hidden = weight_gate.shape[1:]
    capacity = 5 * rows * TOPK // (4 * exp)
    pad = 16 * -(-capacity // 16)
    slots = exp * capacity
    part_width = width // exp
    key_width = max(part_width, HEAD_DIM)
    group = key_width // part_width
    heads = key_width // HEAD_DIM
    span = rows * exp
    scale = 1.0 / math.sqrt(HEAD_DIM * span * ctx)
    me = lax.axis_index(CTX).astype(jnp.int32).reshape(1)
    state_low = shape((heads, HEAD_DIM, part_width // heads), BF16)

    outgoing, query, key = run(
        functools.partial(route_kernel, ctx, exp, group, capacity, pad),
        [
            shape((ctx * exp, capacity, slice_width), BF16),
            shape((exp, rows, key_width), BF16),
            shape((exp, rows + FACTS, key_width), BF16),
        ],
        [expert_ids, gate_weights, tokens, attn_queries, attn_keys],
    )
    doubling = [1 << n for n in range((ctx - 1).bit_length())]

    downs = {0: weight_down[0]}
    for distance in reversed(doubling):
        downs[distance] = swap(weight_down[0], distance)

    straight = [downs[d] for d in doubling]

    query = move(query, "exp").reshape(span, key_width)
    key, query = lax.optimization_barrier((key, query))
    (after,) = run(functools.partial(after_kernel, heads), [state_low], [query, grad_out])
    after_in = [
        lax.ppermute(after, CTX, [(i + step, i) for i in range(ctx - step)]) for step in range(1, ctx)
    ]
    key = move(key, "exp")
    outgoing, key, straight = lax.optimization_barrier((outgoing, key, straight))
    incoming = move(outgoing, ALL)
    downs = spread_rest({0: downs[0], **dict(zip(doubling, straight, strict=True))}, doubling)
    rest = [downs[o] for o in range(1, ctx) if o & (o - 1)]

    terms = run(
        functools.partial(project_kernel, ctx, exp, capacity, pad),
        [shape((slots, 2 * hidden), BF16 if o & 1 else F32) for o in range(ctx)],
        [me, incoming, weight_gate[0], weight_up[0]],
        scratch=[
            pltpu.VMEM((exp * pad, slice_width), BF16),
            pltpu.VMEM((ctx * slots, slice_width), BF16),
        ],
        us=4,
    )
    terms, rest = sum_own(terms, rest)
    downs.update(zip((o for o in range(1, ctx) if o & (o - 1)), rest, strict=True))
    downs = [downs[o] for o in range(ctx)]

    grad_rows, after_low = run(
        functools.partial(grad_values_kernel, heads, capacity, scale),
        [
            shape((exp, slots, part_width), BF16),
            shape((span // BLOCK * heads, HEAD_DIM, part_width // heads), BF16),
        ],
        [query, key, grad_out, *after_in],
        scratch=[pltpu.VMEM((span, part_width), BF16)],
        us=3,
    )
    grad_rows = move(grad_rows, "exp")

    grads, active = run(
        functools.partial(gates_kernel, len(terms)),
        [shape((slots, 2 * hidden), BF16), shape((slots, hidden), BF16)],
        [me, grad_rows, *terms, *downs],
        scratch=[pltpu.VMEM((slots, width), BF16)],
        us=0,
    )
    chunks = {0: grads, **{d: swap(grads, d) for d in reversed(doubling)}}
    (expert_out,) = run(
        forward_kernel,
        [shape((exp, slots, part_width), BF16)],
        [me, active, *downs],
        us=0,
    )
    grad_key, query_part, state = run(
        functools.partial(grad_heads_kernel, heads, capacity, scale),
        [shape((span, key_width), BF16), shape((span, key_width), F32), state_low],
        [query, key, grad_out, after_low, move(expert_out, "exp")],
        us=0,
    )
    state_in = [
        lax.ppermute(state, CTX, [(i, i + step) for i in range(ctx - step)]) for step in range(1, ctx)
    ]
    chunks, state_in = lax.optimization_barrier((chunks, state_in))
    chunks = spread_rest(chunks, doubling)
    chunks = [chunks[o] for o in range(ctx)]
    (outgoing,) = run(
        functools.partial(backward_kernel, ctx, exp, capacity, pad),
        [shape((ctx * exp, capacity, slice_width), BF16)],
        [me, weight_gate[0], weight_up[0], *chunks],
        scratch=[pltpu.VMEM((ctx * slots, 2 * hidden), BF16)],
        us=60,
    )
    (heads_back,) = run(
        functools.partial(finish_kernel, heads, scale),
        [shape((2 * exp, rows, key_width), BF16)],
        [grad_out, query_part, grad_key, *state_in],
        us=0,
    )
    heads_back = move(heads_back.reshape(exp, 2 * rows, key_width), "exp")
    home = move(outgoing, ALL)
    grad_queries, grad_keys = run(
        functools.partial(heads_kernel, group), [shape((rows, width), BF16)] * 2, [heads_back]
    )
    (grad_tokens,) = run(
        functools.partial(home_kernel, ctx, exp, capacity, pad),
        [shape((rows, width), BF16)],
        [expert_ids, gate_weights, home],
        scratch=[pltpu.VMEM((exp * pad, width), BF16)],
    )
    return grad_tokens, grad_queries, grad_keys


def solution(mesh):
    ctx, exp = mesh.shape["ctx"], mesh.shape["exp"]
    lo = 2 if ctx % 2 == 0 else 1
    split = Mesh(mesh.devices.reshape(ctx // lo, lo, exp), ("hi", "lo", "exp"))
    rows, span = P(("hi", "lo", "exp"), None), ("hi", "lo")
    in_specs = (
        rows,
        rows,
        rows,
        P("exp", span, None),
        P("exp", span, None),
        P("exp", None, span),
        rows,
        rows,
        P(span, "exp"),
    )
    return jax.shard_map(
        shards, mesh=split, in_specs=in_specs, out_specs=(rows, rows, rows), check_vma=False
    )
```

```python
import functools
import math

import jax
import jax.numpy as jnp
from jax import lax
from jax.experimental import pallas as pl
from jax.experimental.pallas import tpu as pltpu
from jax.sharding import Mesh
from jax.sharding import PartitionSpec as P

HEAD_DIM = 128
TOPK = 1
BLOCK = 512
VMEM_LIMIT = 32 * 1024 * 1024
BF16 = jnp.bfloat16
F32 = jnp.float32


def dot(left, right):
    return jnp.dot(left, right, preferred_element_type=F32)


def dot_nt(left, right):
    return lax.dot_general(left, right, (((1,), (1,)), ((), ())), preferred_element_type=F32)


def dot_tn(left, right):
    return lax.dot_general(left, right, (((0,), (0,)), ((), ())), preferred_element_type=F32)


def iota(shape, axis):
    return lax.broadcasted_iota(jnp.int32, shape, axis)


def run(kernel, outs, args, scratch=(), us=1):
    in_specs = [
        pl.BlockSpec(memory_space=pltpu.SMEM if a.dtype == jnp.int32 and a.ndim == 1 else pltpu.VMEM)
        for a in args
    ]
    moved = sum(math.prod(a.shape) * a.dtype.itemsize for a in (*args, *outs))
    return pl.pallas_call(
        kernel,
        out_shape=tuple(outs),
        in_specs=in_specs,
        out_specs=tuple(pl.BlockSpec(memory_space=pltpu.VMEM) for _ in outs),
        scratch_shapes=list(scratch),
        compiler_params=pltpu.CompilerParams(vmem_limit_bytes=VMEM_LIMIT),
        cost_estimate=pl.CostEstimate(flops=int(us * 1.15e9), bytes_accessed=moved // 100, transcendentals=0),
    )(*args)


def shape(dims, dtype):
    return jax.ShapeDtypeStruct(dims, dtype)


def row_slots(ids, pad, wide):
    rows = ids.shape[0]
    named = ids == iota((rows, 128 * -(-wide // 128)), 1)
    earlier = (iota((rows, rows), 1) < iota((rows, rows), 0)).astype(BF16)
    counts = dot(earlier, named.astype(BF16))
    rank = jnp.sum(jnp.where(named, counts, 0.0), axis=1, keepdims=True).astype(jnp.int32)
    chosen = (ids * pad + rank == iota((rows, wide * pad), 1)).astype(BF16)
    return rank, chosen


def packing(experts, capacity, pad):
    slots = experts * capacity
    row, col = iota((slots, experts * pad), 0), iota((slots, experts * pad), 1)
    expert = col // pad
    inner = col - expert * pad
    return ((inner < capacity) & (row == expert * capacity + inner)).astype(BF16)


def unpacking(experts, capacity, pad):
    slots = experts * capacity
    row, col = iota((experts * pad, slots), 0), iota((experts * pad, slots), 1)
    expert = row // pad
    inner = row - expert * pad
    return ((inner < capacity) & (col == expert * capacity + inner)).astype(BF16)


FACTS = 16


def route_kernel(
    hi, exp, group, capacity, pad, ids_ref, gate_ref, tokens_ref, query_ref, key_ref, out_ref, query_out, key_out
):
    rows, width = tokens_ref.shape
    part = width // hi
    ids = ids_ref[...]
    rank, chosen = row_slots(ids, pad, exp)
    slot_rows = dot_tn(chosen, tokens_ref[...]).astype(BF16)
    for c in range(hi):
        for e in range(exp):
            out_ref[c * exp + e] = slot_rows[e * pad : e * pad + capacity, c * part : (c + 1) * part]
    gate = gate_ref[...]
    high = gate.astype(BF16).astype(F32)
    mid = (gate - high).astype(BF16).astype(F32)
    lane = iota((rows, 128), 1)
    facts = jnp.zeros((rows, 128), F32)
    for col, fact in enumerate((ids.astype(F32), rank.astype(F32), high, mid, gate - high - mid)):
        facts = jnp.where(lane == col, fact, facts)
    facts = facts.T[:FACTS].astype(BF16)
    key_width = key_out.shape[2]
    for e in range(exp):
        cols = slice(e // group * key_width, (e // group + 1) * key_width)
        query_out[e] = query_ref[:, cols]
        key_out[e, :rows] = key_ref[:, cols]
        key_out[e, rows:] = jnp.zeros((FACTS, key_width), BF16)
        key_out[e, rows:, :rows] = facts


def facts_of(key_ref, source):
    rows = key_ref.shape[1] - FACTS
    return key_ref[source, rows:, :rows].astype(F32)


def key_rows(key_ref, block, cols):
    rows = key_ref.shape[1] - FACTS
    each = BLOCK // rows
    return jnp.concatenate([key_ref[s, :rows, cols] for s in range(block * each, (block + 1) * each)], axis=0)


def slice_cols(index, width):
    return pl.ds(pl.multiple_of(index * width, 128), width)


def project_kernel(ctx, exp, capacity, pad, me_ref, in_ref, gate_ref, up_ref, *rest):
    out_refs, (padded, packed) = rest[:-2], rest[-2:]
    slots = exp * capacity
    hidden = gate_ref.shape[1]
    select = packing(exp, capacity, pad)
    padded[...] = jnp.zeros_like(padded)
    for offset in range(ctx):
        chunk = me_ref[0] ^ offset
        for e in range(exp):
            padded[e * pad : e * pad + capacity, :] = in_ref[chunk * exp + e]
        packed[offset * slots : (offset + 1) * slots, :] = dot(select, padded[...]).astype(BF16)
    for col, weight in enumerate((gate_ref, up_ref)):
        product = dot(packed[...], weight[...])
        for offset in range(ctx):
            out_refs[offset][:, col * hidden : (col + 1) * hidden] = product[
                offset * slots : (offset + 1) * slots
            ].astype(out_refs[offset].dtype)


def gates_kernel(terms, me_ref, grads_ref, *rest):
    sums, downs, (out_ref, active_ref, rows) = rest[:terms], rest[terms:-3], rest[-3:]
    hidden, depth = downs[0].shape
    parts, _, part = grads_ref.shape
    for e in range(parts):
        rows[:, e * part : (e + 1) * part] = grads_ref[e]
    projected = sums[0][...]
    for other in sums[1:]:
        projected = projected + other[...].astype(F32)
    gate, up = projected[:, :hidden], projected[:, hidden:]
    sigmoid = jax.nn.sigmoid(gate)
    active = gate * sigmoid
    active_ref[...] = (active * up).astype(BF16)
    grad = 0.0
    for o, down in enumerate(downs):
        grad += dot_nt(rows[:, slice_cols(me_ref[0] ^ o if len(downs) > 1 else 0, depth)], down[...])
    out_ref[:, :hidden] = (grad * up * (sigmoid * (1.0 + gate * (1.0 - sigmoid)))).astype(BF16)
    out_ref[:, hidden:] = (grad * active).astype(BF16)


def forward_kernel(me_ref, active_ref, *rest):
    downs, out_ref = rest[:-1], rest[-1]
    parts, _, part = out_ref.shape
    each = parts // len(downs)
    for o, down in enumerate(downs):
        product = dot(active_ref[...], down[...]).astype(BF16)
        for b in range(each):
            place = (me_ref[0] ^ o) * each + b if len(downs) > 1 else b
            out_ref[place] = product[:, b * part : (b + 1) * part]


def backward_kernel(exp, capacity, pad, offsets, me_ref, gate_ref, up_ref, *rest):
    count = len(offsets)
    chunks, before, (out_ref, grads) = rest[:count], rest[count:-2], rest[-2:]
    hidden = gate_ref.shape[1]
    slots = exp * capacity
    for ref in before:
        out_ref[...] = ref[...]
    for n in range(count):
        grads[n * slots : (n + 1) * slots, :] = chunks[n][...]
    product = (dot_nt(grads[:, :hidden], gate_ref[...]) + dot_nt(grads[:, hidden:], up_ref[...])).astype(BF16)
    spread = unpacking(exp, capacity, pad)
    for n, offset in enumerate(offsets):
        chunk = me_ref[0] ^ offset
        rows = dot(spread, product[n * slots : (n + 1) * slots]).astype(BF16)
        for e in range(exp):
            out_ref[chunk * exp + e] = rows[e * pad : e * pad + capacity]


def home_kernel(ctx, exp, capacity, pad, ids_ref, gate_ref, in_ref, out_ref, padded):
    part = in_ref.shape[2]
    rank, chosen = row_slots(ids_ref[...], pad, exp)
    padded[...] = jnp.zeros_like(padded)
    for c in range(ctx):
        for e in range(exp):
            padded[e * pad : e * pad + capacity, c * part : (c + 1) * part] = in_ref[c * exp + e]
    out_ref[...] = (gate_ref[...] * dot(chosen, padded[...])).astype(BF16)


def row_place(ids, rank, source, capacity, slots):
    return ids * slots + source * capacity + rank


def after_kernel(heads, query_ref, cot_ref, out_ref):
    width = cot_ref.shape[1] // heads
    for h in range(heads):
        out_ref[h] = dot_tn(
            query_ref[:, h * HEAD_DIM : (h + 1) * HEAD_DIM], cot_ref[:, h * width : (h + 1) * width]
        ).astype(BF16)


def grad_values_kernel(heads, capacity, scale, query_ref, key_ref, cot_ref, *rest):
    arrived, (out_ref, low_ref, grads) = rest[:-3], rest[-3:]
    span, total = cot_ref.shape
    width = total // heads
    blocks = span // BLOCK
    causal = iota((BLOCK, BLOCK), 0) >= iota((BLOCK, BLOCK), 1)
    for h in range(heads):
        keys, cols = slice(h * HEAD_DIM, (h + 1) * HEAD_DIM), slice(h * width, (h + 1) * width)
        state = arrived[0][h].astype(F32)
        for other in arrived[1:]:
            state = state + other[h].astype(F32)
        for n in reversed(range(blocks)):
            rows = slice(n * BLOCK, (n + 1) * BLOCK)
            low = state.astype(BF16)
            low_ref[n * heads + h] = low
            query, key, cot = query_ref[rows, keys], key_rows(key_ref, n, keys), cot_ref[rows, cols]
            scores = jnp.where(causal, dot_nt(query, key), 0.0).astype(BF16)
            grads[rows, cols] = (scale * (dot_tn(scores, cot) + dot(key, low))).astype(BF16)
            if n:
                state = state + dot_tn(query, cot)
    sources, slots = key_ref.shape[0], out_ref.shape[1]
    facts = [facts_of(key_ref, s) for s in range(sources)]
    place = jnp.concatenate(
        [
            row_place(
                facts[s][0:1].astype(jnp.int32), facts[s][1:2].astype(jnp.int32), s, capacity, slots
            )
            for s in range(sources)
        ],
        axis=1,
    )
    row = iota((slots, span), 0)
    for e in range(out_ref.shape[0]):
        chosen = (place == row + e * slots).astype(BF16)
        out_ref[e] = dot(chosen, grads[...]).astype(BF16)


def grad_heads_kernel(
    heads, capacity, scale, query_ref, key_ref, cot_ref, low_ref, in_ref, key_out, part_out, state_out
):
    span, total = cot_ref.shape
    width = total // heads
    blocks = span // BLOCK
    slots = in_ref.shape[1]
    rows_each = key_ref.shape[1] - FACTS
    returned = in_ref[...].reshape(-1, total)
    causal = iota((BLOCK, BLOCK), 0) >= iota((BLOCK, BLOCK), 1)
    states = [jnp.zeros((HEAD_DIM, width), F32) for _ in range(heads)]
    for n in range(blocks):
        rows = slice(n * BLOCK, (n + 1) * BLOCK)
        places, weights = [], []
        for s in range(n * BLOCK // rows_each, (n + 1) * BLOCK // rows_each):
            facts = facts_of(key_ref, s).T
            places.append(
                row_place(
                    facts[:, 0:1].astype(jnp.int32), facts[:, 1:2].astype(jnp.int32), s, capacity, slots
                )
            )
            weights.append(facts[:, 2:3] + facts[:, 3:4] + facts[:, 4:5])
        place, weight = jnp.concatenate(places, axis=0), jnp.concatenate(weights, axis=0)
        chosen = (place == iota((BLOCK, returned.shape[0]), 1)).astype(BF16)
        values = (weight * dot(chosen, returned)).astype(BF16)
        for h in range(heads):
            keys, cols = slice(h * HEAD_DIM, (h + 1) * HEAD_DIM), slice(h * width, (h + 1) * width)
            query, key, cot = query_ref[rows, keys], key_rows(key_ref, n, keys), cot_ref[rows, cols]
            value = values[:, cols]
            probes = jnp.where(causal, dot_nt(cot, value), 0.0).astype(BF16)
            key_out[rows, keys] = (
                scale * (dot_tn(probes, query) + dot_nt(value, low_ref[n * heads + h]))
            ).astype(BF16)
            part = dot(probes, key)
            if n:
                part = part + dot_nt(cot, states[h].astype(BF16))
            part_out[rows, keys] = part
            states[h] = states[h] + dot_tn(key, value)
    for h in range(heads):
        state_out[h] = states[h].astype(BF16)


def finish_kernel(heads, scale, cot_ref, part_ref, grad_key_ref, *rest):
    arrived, out_ref = rest[:-1], rest[-1]
    width = cot_ref.shape[1] // heads
    sources, rows = out_ref.shape[0] // 2, out_ref.shape[1]
    for h in range(heads):
        keys, cols = slice(h * HEAD_DIM, (h + 1) * HEAD_DIM), slice(h * width, (h + 1) * width)
        state = arrived[0][h].astype(F32)
        for other in arrived[1:]:
            state = state + other[h].astype(F32)
        grad = (scale * (part_ref[:, keys] + dot_nt(cot_ref[:, cols], state.astype(BF16)))).astype(BF16)
        for s in range(sources):
            out_ref[2 * s, :, keys] = grad[s * rows : (s + 1) * rows]
    for s in range(sources):
        out_ref[2 * s + 1] = grad_key_ref[s * rows : (s + 1) * rows]


def heads_kernel(group, in_ref, query_ref, key_ref):
    sources, both, key_width = in_ref.shape
    rows = both // 2
    for n in range(sources // group):
        for place, out in enumerate((query_ref, key_ref)):
            inner = slice(place * rows, (place + 1) * rows)
            total = in_ref[n * group, inner]
            if group > 1:
                total = total.astype(F32)
                for part in range(1, group):
                    total = total + in_ref[n * group + part, inner].astype(F32)
            out[:, n * key_width : (n + 1) * key_width] = total.astype(BF16)


def move(buffer, axes):
    return lax.all_to_all(buffer, axes, split_axis=0, concat_axis=0, tiled=True)


CTX = ("hi", "lo")
ALL = ("hi", "lo", "exp")


def swap(block, distance):
    count = lax.axis_size("hi") * lax.axis_size("lo")
    return lax.ppermute(block, CTX, [(i, i ^ distance) for i in range(count)])


def spread_rest(chunks, distances):
    chunks = dict(chunks)
    for distance in sorted(distances, reverse=True):
        for o in [o for o in chunks if not o & distance and o and o | distance not in chunks and o > distance]:
            chunks[o | distance] = swap(chunks[o], distance)
    return chunks


def sum_own(terms, rest):
    count, distance = len(terms), 1
    held, own = dict(enumerate(terms)), [terms[0]]
    while distance < count:
        urgent = sorted((o for o in held if o & distance and o != distance), reverse=True)
        arrived = {o ^ distance: swap(held[o].astype(BF16), distance) for o in urgent}
        last = held[distance].astype(BF16)
        held = {o: held[o].astype(F32) + term.astype(F32) for o, term in arrived.items()}
        if distance == 1:
            last, rest = lax.optimization_barrier((last, rest))
        own.append(swap(last, distance))
        distance *= 2
    return own, rest


def shards(
    tokens,
    expert_ids,
    gate_weights,
    weight_gate,
    weight_up,
    weight_down,
    attn_queries,
    attn_keys,
    grad_out,
):
    exp, hi, lo = lax.axis_size("exp"), lax.axis_size("hi"), lax.axis_size("lo")
    ctx = hi * lo
    rows, width = tokens.shape
    slice_width, hidden = weight_gate.shape[1:]
    capacity = 5 * rows * TOPK // (4 * exp)
    pad = 16 * -(-capacity // 16)
    slots = exp * capacity
    part_width = width // exp
    key_width = max(part_width, HEAD_DIM)
    group = key_width // part_width
    heads = key_width // HEAD_DIM
    span = rows * exp
    scale = 1.0 / math.sqrt(HEAD_DIM * span * ctx)
    me = lax.axis_index(CTX).astype(jnp.int32).reshape(1)
    state_low = shape((heads, HEAD_DIM, part_width // heads), BF16)

    outgoing, query, key = run(
        functools.partial(route_kernel, ctx, exp, group, capacity, pad),
        [
            shape((ctx * exp, capacity, slice_width), BF16),
            shape((exp, rows, key_width), BF16),
            shape((exp, rows + FACTS, key_width), BF16),
        ],
        [expert_ids, gate_weights, tokens, attn_queries, attn_keys],
    )
    doubling = [1 << n for n in range((ctx - 1).bit_length())]

    downs = {0: weight_down[0]}
    for distance in reversed(doubling):
        downs[distance] = swap(weight_down[0], distance)

    straight = [downs[d] for d in doubling]

    query = move(query, "exp").reshape(span, key_width)
    key, query = lax.optimization_barrier((key, query))
    (after,) = run(functools.partial(after_kernel, heads), [state_low], [query, grad_out])
    after_in = [
        lax.ppermute(after, CTX, [(i + step, i) for i in range(ctx - step)]) for step in range(1, ctx)
    ]
    key = move(key, "exp")
    outgoing, key, straight = lax.optimization_barrier((outgoing, key, straight))
    incoming = move(outgoing, ALL)
    downs = spread_rest({0: downs[0], **dict(zip(doubling, straight, strict=True))}, doubling)
    rest = [downs[o] for o in range(1, ctx) if o & (o - 1)]

    terms = run(
        functools.partial(project_kernel, ctx, exp, capacity, pad),
        [shape((slots, 2 * hidden), BF16 if o & 1 else F32) for o in range(ctx)],
        [me, incoming, weight_gate[0], weight_up[0]],
        scratch=[
            pltpu.VMEM((exp * pad, slice_width), BF16),
            pltpu.VMEM((ctx * slots, slice_width), BF16),
        ],
        us=4,
    )
    terms, rest = sum_own(terms, rest)
    downs.update(zip((o for o in range(1, ctx) if o & (o - 1)), rest, strict=True))
    downs = [downs[o] for o in range(ctx)]

    grad_rows, after_low = run(
        functools.partial(grad_values_kernel, heads, capacity, scale),
        [
            shape((exp, slots, part_width), BF16),
            shape((span // BLOCK * heads, HEAD_DIM, part_width // heads), BF16),
        ],
        [query, key, grad_out, *after_in],
        scratch=[pltpu.VMEM((span, part_width), BF16)],
        us=3,
    )
    grad_rows = move(grad_rows, "exp")

    grads, active = run(
        functools.partial(gates_kernel, len(terms)),
        [shape((slots, 2 * hidden), BF16), shape((slots, hidden), BF16)],
        [me, grad_rows, *terms, *downs],
        scratch=[pltpu.VMEM((slots, width), BF16)],
        us=0,
    )
    chunks = {0: grads, **{d: swap(grads, d) for d in reversed(doubling)}}
    (expert_out,) = run(
        forward_kernel,
        [shape((exp, slots, part_width), BF16)],
        [me, active, *downs],
        us=0,
    )
    grad_key, query_part, state = run(
        functools.partial(grad_heads_kernel, heads, capacity, scale),
        [shape((span, key_width), BF16), shape((span, key_width), F32), state_low],
        [query, key, grad_out, after_low, move(expert_out, "exp")],
        us=0,
    )
    state_in = [
        lax.ppermute(state, CTX, [(i, i + step) for i in range(ctx - step)]) for step in range(1, ctx)
    ]
    chunks, state_in = lax.optimization_barrier((chunks, state_in))
    chunks = spread_rest(chunks, doubling)
    chunks = [chunks[o] for o in range(ctx)]
    before = []
    for offsets in (tuple(range(ctx - 1)), (ctx - 1,)):
        before = run(
            functools.partial(backward_kernel, exp, capacity, pad, offsets),
            [shape((ctx * exp, capacity, slice_width), BF16)],
            [me, weight_gate[0], weight_up[0], *(chunks[o] for o in offsets), *before],
            scratch=[pltpu.VMEM((len(offsets) * slots, 2 * hidden), BF16)],
            us=60 if len(offsets) == 1 else 3,
        )
    (outgoing,) = before
    (heads_back,) = run(
        functools.partial(finish_kernel, heads, scale),
        [shape((2 * exp, rows, key_width), BF16)],
        [grad_out, query_part, grad_key, *state_in],
        us=0,
    )
    heads_back = move(heads_back.reshape(exp, 2 * rows, key_width), "exp")
    home = move(outgoing, ALL)
    grad_queries, grad_keys = run(
        functools.partial(heads_kernel, group), [shape((rows, width), BF16)] * 2, [heads_back]
    )
    (grad_tokens,) = run(
        functools.partial(home_kernel, ctx, exp, capacity, pad),
        [shape((rows, width), BF16)],
        [expert_ids, gate_weights, home],
        scratch=[pltpu.VMEM((exp * pad, width), BF16)],
    )
    return grad_tokens, grad_queries, grad_keys


def solution(mesh):
    ctx, exp = mesh.shape["ctx"], mesh.shape["exp"]
    lo = 2 if ctx % 2 == 0 else 1
    split = Mesh(mesh.devices.reshape(ctx // lo, lo, exp), ("hi", "lo", "exp"))
    rows, span = P(("hi", "lo", "exp"), None), ("hi", "lo")
    in_specs = (
        rows,
        rows,
        rows,
        P("exp", span, None),
        P("exp", span, None),
        P("exp", None, span),
        rows,
        rows,
        P(span, "exp"),
    )
    return jax.shard_map(
        shards, mesh=split, in_specs=in_specs, out_specs=(rows, rows, rows), check_vma=False
    )
```
